512 devices in a mesh: group: 4 (over y_lo, core), fsdp: 8 (over x, y_hi), tensor: 16 (over z).
Axes of the slice: x: 4, y: 4 (y_hi: 2, y_lo: 2; y = y_hi * 2 + y_lo), z: 16, core: 2. Of those that a mesh axis runs over, the one named last changes fastest.
Arguments:
- tokens_in: bfloat16 [12288, 8192], P(('group', 'fsdp'), 'tensor'), may hold values from -6 to 6
- norm_gain: bfloat16 [8192], P('tensor'), may hold values from 0.099609375 to 1.8984375
- segment_ids: int32 [4, 3072], P('group'), may hold values from 0 to 3, never falling along the last dimension, each value on 1 to 1536 neighbouring positions
- wq: float32 [8192, 8192], P(('group', 'fsdp', 'tensor')), may hold values from -0.22097087 to 0.22097087
- wk: float32 [8192, 1024], P(('group', 'fsdp', 'tensor')), may hold values from -0.22097087 to 0.22097087
- wv: float32 [8192, 1024], P(('group', 'fsdp', 'tensor')), may hold values from -0.25 to 0.25
Outputs:
- attended: bfloat16 [12288, 8192], P(('group', 'fsdp'), 'tensor')
The draws below stay inside these ranges and needn't reach their ends.
Inputs may be any that keep to these rules, and one draw needn't show every extreme that they name: segment_ids numbers the documents of each prompt, never falling along the prompt; each prompt holds 4 documents of 1 to 1536 tokens, one of exactly 1536.
All inputs are finite; a program needn't handle non-finite values.
Results may differ from the reference program's by a relative error of at most 0.012.
Values may be sent and summed in bfloat16 or wider, within the bound.
A program may use at most 64 MiB of HBM per device.

```python
import math
import jax
import jax.numpy as jnp
import numpy as np
from jax import lax

D = 8192
HD = 128
QPK = 8
KV = 8
HQ = 64
DOCS = 4
SEQ = 3072
TOKENS = 12288
N_GROUP = 4
N_FSDP = 8
N_TENSOR = 16


def spike_factor(key, columns):
    row_blocks = N_GROUP * N_FSDP * N_TENSOR
    picks = jax.random.randint(key, (row_blocks,), 0, N_TENSOR)
    row_pick = jnp.repeat(picks, D // row_blocks)[:, None]
    col_block = (jnp.arange(columns, dtype=jnp.int32) // (columns // N_TENSOR))[None, :]
    return jnp.where(row_pick == col_block, 3.0, 1.0).astype(jnp.float32)


def draw_wq(key, part):
    key = jax.random.fold_in(key, 11)
    columns = HQ * HD
    factor = spike_factor(jax.random.fold_in(key, 1), columns)
    base = jax.random.truncated_normal(jax.random.fold_in(key, 2), -6.0, 6.0, (D, columns), jnp.float32)
    limit = 20.0 / math.sqrt(D)
    return jnp.clip(base * factor / math.sqrt(D), -limit, limit)


def draw_wk(key, part):
    key = jax.random.fold_in(key, 12)
    columns = KV * HD
    factor = spike_factor(jax.random.fold_in(key, 1), columns)
    base = jax.random.truncated_normal(jax.random.fold_in(key, 2), -6.0, 6.0, (D, columns), jnp.float32)
    limit = 20.0 / math.sqrt(D)
    return jnp.clip(base * factor / math.sqrt(D), -limit, limit)


def draw_tokens_in(key, part):
    key = jax.random.fold_in(key, 13)
    rows = jax.random.truncated_normal(jax.random.fold_in(key, 1), -6.0, 6.0, (TOKENS, D), jnp.float32)
    return jnp.clip(rows, -6.0, 6.0).astype(jnp.bfloat16)


def strengthened(drawn, stream_key, source, target, shards_of, factor):
    owner, partner = [(jnp.arange(drawn.shape[dim]) // (drawn.shape[dim] // shards_of)).reshape([-1 if axis == dim else 1 for axis in range(drawn.ndim)]) for dim in (source, target)]
    chosen = jax.random.permutation(stream_key, shards_of)[partner]
    strong = (owner == chosen) | (owner == (partner + shards_of // 2) % shards_of)
    return jnp.where(strong, factor * drawn, drawn)


def steps_of(key, shape, split, least, largest):
    gain = 1.0
    for position, parts in split:
        draws = jax.random.uniform(jax.random.fold_in(jax.random.fold_in(key, 6), position), (parts,), jnp.float32, least / len(split), largest / len(split))
        gain = gain * jnp.repeat(jnp.exp(draws), shape[position] // parts).reshape((-1,) + (1,) * (len(shape) - 1 - position))
    return gain


def split_up(amount, total, most, slope):
    weights = [(1 << 20) // math.isqrt(standing ** slope) + 1 for standing in range(2, amount + 1)]
    surplus, counts = total - most - (amount - 1), [1] * (amount - 1)
    while surplus > 0:
        movable = [i for i in range(amount - 1) if counts[i] < most]
        pool, budget = sum([weights[i] for i in movable]), surplus
        for i in movable:
            more = min(most - counts[i], max(1, budget * weights[i] // pool), surplus)
            counts[i] = counts[i] + more
            surplus = surplus - more
    return np.array([most] + counts)


def ragged(own_key, count, total, most, skew):
    if count == 2:
        one = jax.random.randint(own_key, (), max(1, total - most), min(most, total - 1) + 1)
        return jnp.stack([one, total - one])
    lengths = jnp.asarray(split_up(count, total, most, skew), jnp.int32)
    pairs = (count - 1) // 2
    giver, sink = lengths[1:1 + 2 * pairs:2], lengths[2:2 + 2 * pairs:2]
    room = jnp.minimum(giver - 1, most - sink)
    moved = jax.random.randint(jax.random.fold_in(own_key, 1), (pairs,), 0, 1 << 20) % (room + 1)
    lengths = lengths.at[1:1 + 2 * pairs:2].set(giver - moved).at[2:2 + 2 * pairs:2].set(sink + moved)
    return lengths[jax.random.permutation(jax.random.fold_in(own_key, 2), count)]


def heavy_noise(key, dims, scale, reach, split, heavy, kind=jnp.bfloat16):
    values = scale * jax.random.normal(key, dims, jnp.float32)
    if split:
        values = values * steps_of(key, dims, split, -0.22, 0.18)
    return jnp.clip(strengthened(values, jax.random.fold_in(key, 3), *heavy), -reach, reach).astype(kind)


def setup_inputs(seed: int = 0) -> dict:
    key_of = jax.random.split(jax.random.key(seed), 7)
    return {
        "tokens_in": draw_tokens_in(jax.random.fold_in(key_of[6], 71), 0),
        "norm_gain": jnp.clip(1.0 + 0.18 * jax.random.normal(key_of[1], (D,), jnp.float32), 0.099609375, 1.8984375).astype(jnp.bfloat16),
        "segment_ids": jax.vmap(lambda own: jnp.searchsorted(jnp.cumsum(ragged(own, DOCS, SEQ, SEQ // 2, 2)), jnp.arange(SEQ), side="right"))(jax.random.split(key_of[2], N_GROUP)).reshape((N_GROUP, SEQ)).astype(jnp.int32),
        "wq": draw_wq(jax.random.fold_in(key_of[6], 71), 0),
        "wk": draw_wk(jax.random.fold_in(key_of[6], 71), 0),
        "wv": heavy_noise(key_of[5], (D, KV * HD), D ** -0.5, 0.25, ((0, 512),), (0, 1, 512, 6.0), jnp.float32),
    }


eps_norm = 1e-05
rope_base = 500000.0

def doc_positions(segments):
    positions = jnp.arange(segments.shape[0], dtype=jnp.int32)
    change = jnp.concatenate([jnp.ones((1,), dtype=bool), segments[1:] != segments[:-1]])
    begins = lax.cummax(jnp.where(change, positions, 0).astype(jnp.int32), axis=0)
    return positions - begins

def rotate(projected, places, heads):
    half_dim = HD // 2
    shaped = projected.reshape(projected.shape[0], heads, HD)
    inv_freq = jnp.power(rope_base, -jnp.arange(half_dim, dtype=jnp.float32) / half_dim)
    angles = places.astype(jnp.float32)[:, None] * inv_freq[None, :]
    cosine = jnp.cos(angles)[:, None, :]
    sine = jnp.sin(angles)[:, None, :]
    front_part = shaped[..., :half_dim]
    back_part = shaped[..., half_dim:]
    return jnp.concatenate([front_part * cosine - back_part * sine, back_part * cosine + front_part * sine], axis=2)

def attend(queries, keys, values, allowed):
    scores = jnp.einsum('qhd,kd->hqk', queries.astype(jnp.float32), keys.astype(jnp.float32)) * HD ** (-0.5)
    masked = jnp.where(allowed[None], scores, -1e+30)
    row_max = lax.optimization_barrier(jnp.max(masked, axis=2, keepdims=True))
    exps = jnp.where(allowed[None], jnp.exp(masked - row_max), 0.0)
    attn_probs = (exps / lax.optimization_barrier(jnp.sum(exps, axis=2, keepdims=True))).astype(jnp.bfloat16)
    return jnp.einsum('hqk,kd->qhd', attn_probs.astype(jnp.float32), values.astype(jnp.float32))

def reference(tokens_in, norm_gain, segment_ids, wq, wk, wv):
    floats = tokens_in.astype(jnp.float32)
    scale_rows = lax.rsqrt(lax.optimization_barrier(jnp.mean(floats * floats, axis=1, keepdims=True)) + eps_norm)
    normed = (floats * scale_rows * norm_gain.astype(jnp.float32)).astype(jnp.bfloat16)
    q_proj = jnp.dot(normed, wq.astype(jnp.bfloat16), preferred_element_type=jnp.float32)
    k_proj = jnp.dot(normed, wk.astype(jnp.bfloat16), preferred_element_type=jnp.float32)
    v_proj = jnp.dot(normed, wv.astype(jnp.bfloat16), preferred_element_type=jnp.float32)
    positions = jnp.arange(SEQ, dtype=jnp.int32)
    outputs = []
    for group_row in range(N_GROUP):
        low_row = group_row * SEQ
        segments = segment_ids[group_row]
        places = doc_positions(segments)
        queries = rotate(q_proj[low_row:low_row + SEQ], places, HQ).astype(jnp.bfloat16).reshape(SEQ, KV, QPK, HD)
        keys = rotate(k_proj[low_row:low_row + SEQ], places, KV).astype(jnp.bfloat16)
        values = v_proj[low_row:low_row + SEQ].astype(jnp.bfloat16).reshape(SEQ, KV, HD)
        allowed = (positions[None, :] <= positions[:, None]) & (segments[None, :] == segments[:, None])

        def one_head(operands):
            return attend(operands[0], operands[1], operands[2], allowed)
        result = lax.map(one_head, (queries.transpose(1, 0, 2, 3), keys.transpose(1, 0, 2), values.transpose(1, 0, 2)))
        outputs.append(result.transpose(1, 0, 2, 3).reshape(SEQ, HQ * HD))
    return jnp.concatenate(outputs, axis=0).astype(jnp.bfloat16)
```

```python
import functools

import jax
import jax.numpy as jnp
import numpy as np
from jax import lax
from jax.experimental import pallas as pl
from jax.experimental.pallas import tpu as pltpu
from jax.sharding import PartitionSpec as P

MESH = pl.DeviceIdType.MESH
F32, BF16 = jnp.float32, jnp.bfloat16
HD = 128
ROWS = 384
FEAT = 512
NZ = 16
CHUNKS, CHUNK = 3, 128
HALF = CHUNK // 2
COLS = 640
BACK = 4
BAND = (BACK + 1) * ROWS
EPS = 1e-05
T_PLANE1, T_PLANE2, T_PLANE3, T_MM = 1, 5, 11, 12


def document_starts(seg):
    return [jnp.sum(jnp.where(seg < d, 1.0, 0.0), axis=1, keepdims=True) for d in (1, 2, 3)]


def start_of(row, begins):
    start = jnp.zeros_like(row)
    for b in begins:
        start = jnp.where(row >= b, b, start)
    return start


def front(tok_ref, gain_ref, seg_ref, freq_ref, wq_ref, wk_ref, wv_ref, q_ref, k_ref, v_ref,
          wsend, wbuf, tok, ssq, acc, trig, kv,
          a_send, a_recv, s_send, s_recv, p_send, p_recv, b_send, b_recv, r_send, r_recv, k_send, k_recv):
    g, f, z = lax.axis_index("group"), lax.axis_index("fsdp"), lax.axis_index("tensor")
    x, y, c = f // 2, (f % 2) * 2 + g // 2, g % 2
    par = z % 2
    mate = z + 1 - 2 * par

    def chip(px, py, core):
        return (py % 2) * 2 + core, px * 2 + py // 2

    def place(first, second, core=None):
        return chip((x + (1 - c) * first + c * second) % 4, (y + c * first + (1 - c) * second) % 4, c)

    def dev(gf, zz):
        return {"group": gf[0], "fsdp": gf[1], "tensor": zz}

    def copy(src, dst, send, recv, to):
        return pltpu.make_async_remote_copy(src_ref=src, dst_ref=dst, send_sem=send, recv_sem=recv, device_id=to, device_id_type=MESH)

    bar = pltpu.get_barrier_semaphore()
    count = 0
    for d in range(1, NZ):
        pl.semaphore_signal(bar, inc=1, device_id=dev((g, f), (z + d) % NZ), device_id_type=MESH)
        count += 1
    for d in (1, 2, 3):
        for to in (place(d, 0), place(0, d)):
            pl.semaphore_signal(bar, inc=1, device_id=dev(to, z), device_id_type=MESH)
            count += 1
    sibling = chip(x, y, 1 - c)
    pl.semaphore_signal(bar, inc=1, device_id=dev(sibling, z), device_id_type=MESH)
    count += 1
    for d in range(1, 8):
        for zz in (z, mate):
            pl.semaphore_signal(bar, inc=1, device_id=dev((g, (f + d) % 8), zz), device_id_type=MESH)
            count += 1

    floats = tok_ref[...].astype(F32)
    part = jnp.sum(floats * floats, axis=1, keepdims=True)
    ssq[z] = jnp.broadcast_to(part, (ROWS, 128)).T[0:1]

    for d in range(NZ):
        wsend[d, :, 0:512] = wq_ref[:, 512 * d:512 * d + 512].astype(BF16)
        side = (wk_ref, wv_ref)[d % 2]
        wsend[d, :, 512:640] = side[:, 128 * (d // 2):128 * (d // 2) + 128].astype(BF16)
    slot = g * 8 + f
    my_rows = pl.ds(pl.multiple_of(z * 16, 16), 16)

    pl.semaphore_wait(bar, count)

    def square(d):
        to = (z + d) % NZ
        return copy(ssq.at[z], ssq.at[z], s_send.at[d], s_recv.at[d], dev((g, f), to))

    def relay(d):
        to = (z + d) % NZ
        return copy(wsend.at[to], wbuf.at[slot, my_rows], a_send.at[d], a_recv.at[d], dev((g, f), to))

    for d in range(1, NZ):
        square(d).start()
    for d in range(1, NZ):
        relay(d).start()
    wbuf[slot, my_rows, :] = wsend[z]

    for d in range(1, BACK + 1):
        @pl.when(f < d)
        def _():
            kv[:, (BACK - d) * ROWS:(BACK - d + 1) * ROWS, :] = jnp.zeros((2, ROWS, HD), BF16)

    begins = document_starts(seg_ref[...])
    row = (lax.broadcasted_iota(jnp.int32, (ROWS, HD), 0) + f * ROWS).astype(F32)
    angle = (row - start_of(row, begins)) * freq_ref[...]
    cosine, sine = jnp.cos(angle), jnp.sin(angle)
    lane = lax.broadcasted_iota(jnp.int32, (ROWS, HD), 1)
    trig[0] = cosine
    trig[1] = jnp.where(lane < HD // 2, -sine, sine)

    for d in range(1, NZ):
        square(d).wait_recv()
    total = jnp.sum(ssq[...], axis=0)
    scale = lax.rsqrt(jnp.broadcast_to(total, (128, ROWS)).T * (1.0 / 8192) + EPS)
    for j in range(FEAT // 128):
        cut = slice(128 * j, 128 * j + 128)
        tok[z, :, cut] = (tok_ref[:, cut].astype(F32) * scale * gain_ref[:, cut].astype(F32)).astype(BF16)

    def hop(ch, step, h, r):
        to = (z + 1 - 2 * r + NZ) % NZ
        owner = (z + NZ + (2 * r - 1) * step) % NZ
        ref = tok.at[owner, pl.ds(pl.multiple_of(ch * CHUNK + h * HALF, HALF), HALF)]
        i = (ch * 8 + step) * 2 + h
        return copy(ref, ref, r_send.at[r, i], r_recv.at[r, i], dev((g, f), to))

    WAYS = ((0, 0), (0, 1), (1, 0), (1, 1))

    def is_long(h, r):
        return h == r

    def ring(ch, step, h):
        for r in (0, 1):
            @pl.when(step > 0)
            def _():
                hop(ch, step - 1, h, r).wait_recv()
            if is_long(h, r):
                hop(ch, step, h, r).start()
            else:
                @pl.when(step < 7)
                def _():
                    hop(ch, step, h, r).start()

    def last_arrivals(ch):
        for h in (0, 1):
            hop(ch, 7, h, h).wait_recv()

    def slot_at(first, second):
        gf = place(first, second)
        return gf[0] * 8 + gf[1]

    def to_first(d):
        ref = wbuf.at[slot]
        return copy(ref, ref, p_send.at[d - 1], p_recv.at[d - 1], dev(place(d, 0), z))

    def to_second(j, d):
        ref = wbuf.at[slot_at(j, 0)]
        i = 3 + j * 3 + d - 1
        return copy(ref, ref, p_send.at[i], p_recv.at[i], dev(place(0, d), z))

    def to_sibling(j, d):
        ref = wbuf.at[slot_at(j, d)]
        i = j * 4 + d
        return copy(ref, ref, b_send.at[i], b_recv.at[i], dev(sibling, z))

    def plane1():
        for d in range(1, NZ):
            relay(d).wait_recv()
        for d in (1, 3, 2):
            to_first(d).start()
        for d in (1, 3, 2):
            to_second(0, d).start()
        to_sibling(0, 0).start()

    def plane2():
        for d in (1, 3, 2):
            to_first(d).wait_recv()
            for e in (1, 3, 2):
                to_second(4 - d, e).start()
            to_sibling(4 - d, 0).start()

    def plane3():
        for j in range(4):
            for d in (1, 3, 2):
                to_second(j, d).wait_recv()
                to_sibling(j, 4 - d).start()
        for j in range(4):
            for d in range(4):
                to_sibling(j, d).wait_recv()

    def multiply(ch, offset, first):
        owner = (z + offset + NZ) % NZ
        rows = pl.ds(pl.multiple_of(ch * CHUNK, CHUNK), CHUNK)
        w = wbuf[pl.ds(owner * 2, 2)].reshape(FEAT, COLS)
        prod = jnp.dot(tok[owner, rows, :], w, preferred_element_type=F32)
        if first:
            acc[rows, :] = prod
        else:
            acc[rows, :] += prod

    def kv_copy(ch, d, other):
        src = kv.at[par, pl.ds(pl.multiple_of(BACK * ROWS + ch * CHUNK, CHUNK), CHUNK)]
        dst = kv.at[par, pl.ds(pl.multiple_of((BACK - d) * ROWS + ch * CHUNK, CHUNK), CHUNK)]
        i = ch * 5 + d
        zz = mate if other else z
        return copy(src, dst, k_send.at[int(other), i], k_recv.at[par, i], dev((g, (f + d) % 8), zz))

    def finish(ch):
        rows = pl.ds(pl.multiple_of(ch * CHUNK, CHUNK), CHUNK)
        cosine, sine = trig[0, rows, :], trig[1, rows, :]
        for h in range(4):
            a = acc[rows, HD * h:HD * h + HD]
            q_ref[rows, HD * h:HD * h + HD] = (a * cosine + pltpu.roll(a, HD // 2, 1) * sine).astype(BF16)
        a = acc[rows, 512:640]
        is_key = par == 0
        rotated = jnp.where(is_key, a * cosine + pltpu.roll(a, HD // 2, 1) * sine, a)
        kv[par, pl.ds(pl.multiple_of(BACK * ROWS + ch * CHUNK, CHUNK), CHUNK), :] = rotated.astype(BF16)
        kv_copy(ch, 0, True).start()
        for d in (4, 3, 2, 1):
            @pl.when(f + d < 8)
            def _():
                kv_copy(ch, d, False).start()
                kv_copy(ch, d, True).start()

    def slot_step(t, _):
        ch, step = t // 8, t % 8
        m = t - T_MM
        mch, quarter = m // 4, m % 4

        def some(n):
            i = quarter * 4 + n
            multiply(mch, (i + 1) // 2 * (2 * (i % 2) - 1), False)

        ring(ch, step, 0)

        @pl.when((t >= T_MM) & (quarter == 0))
        def _():
            rows = pl.ds(pl.multiple_of(mch * CHUNK, CHUNK), CHUNK)
            acc[rows, :] = jnp.zeros((CHUNK, COLS), F32)

        @pl.when(t >= T_MM)
        def _():
            some(0)

        ring(ch, step, 1)

        @pl.when(t >= T_MM)
        def _():
            some(1)
            some(2)

            @pl.when(t < CHUNKS * 8 - 1)
            def _():
                some(3)

        @pl.when(t == T_PLANE1)
        def _():
            plane1()

        @pl.when(t == T_PLANE2)
        def _():
            plane2()

        @pl.when(t == T_PLANE3)
        def _():
            plane3()

        @pl.when((step == 1) & (ch > 0))
        def _():
            last_arrivals(ch - 1)

        @pl.when((t >= T_MM) & (quarter == 3) & (mch < CHUNKS - 1))
        def _():
            finish(mch)
        return 0

    lax.fori_loop(0, CHUNKS * 8, slot_step, 0)
    last_arrivals(CHUNKS - 1)
    multiply(CHUNKS - 1, 8, False)
    finish(CHUNKS - 1)

    def kv_wait(kind, ch, d):
        dst = kv.at[kind, pl.ds((BACK - d) * ROWS + ch * CHUNK, CHUNK)]
        i = ch * 5 + d
        copy(dst, dst, k_send.at[0, i], k_recv.at[kind, i], dev((g, f), z)).wait_recv()

    for ch in range(CHUNKS):
        kv_wait(1 - par, ch, 0)
        for d in range(1, BACK + 1):
            @pl.when(f >= d)
            def _():
                kv_wait(0, ch, d)
                kv_wait(1, ch, d)
    k_ref[...] = kv[0]
    v_ref[...] = kv[1]

    for d in range(1, NZ):
        square(d).wait_send()
        relay(d).wait_send()
    for d in (1, 2, 3):
        to_first(d).wait_send()
    for j in range(4):
        for d in (1, 2, 3):
            to_second(j, d).wait_send()
        for d in range(4):
            to_sibling(j, d).wait_send()

    def drain(t, _):
        ch, step = t // 8, t % 8
        for h, r in WAYS:
            if is_long(h, r):
                hop(ch, step, h, r).wait_send()
            else:
                @pl.when(step < 7)
                def _():
                    hop(ch, step, h, r).wait_send()
        return 0

    lax.fori_loop(0, CHUNKS * 8, drain, 0)
    for ch in range(CHUNKS):
        kv_copy(ch, 0, True).wait_send()
        for d in (4, 3, 2, 1):
            @pl.when(f + d < 8)
            def _():
                kv_copy(ch, d, False).wait_send()
                kv_copy(ch, d, True).wait_send()


def attend(q_ref, k_ref, v_ref, seg_ref, o_ref, bias):
    f = lax.axis_index("fsdp")
    begins = document_starts(seg_ref[...])
    width = BACK * ROWS + CHUNK
    for i in range(CHUNKS):
        rows = slice(i * CHUNK, (i + 1) * CHUNK)
        keys = slice(i * CHUNK, i * CHUNK + width)
        q_at = (lax.broadcasted_iota(jnp.int32, (CHUNK, 128), 0) + (f * ROWS + i * CHUNK)).astype(F32)
        start = start_of(q_at, begins)
        for j in range(width // 128):
            k_at = (lax.broadcasted_iota(jnp.int32, (CHUNK, 128), 1) + ((f - BACK) * ROWS + i * CHUNK + j * 128)).astype(F32)
            bias[:, 128 * j:128 * j + 128] = jnp.where((k_at >= start) & (k_at <= q_at), 0.0, -1e30)
        for h in range(4):
            cols = slice(HD * h, HD * h + HD)
            s = lax.dot_general(q_ref[rows, cols], k_ref[keys, :], (((1,), (1,)), ((), ())), preferred_element_type=F32)
            s = s * HD ** (-0.5) + bias[...]
            p = jnp.exp(s - jnp.max(s, axis=1, keepdims=True))
            total = jnp.sum(p, axis=1, keepdims=True)
            o = jnp.dot(p.astype(BF16), v_ref[keys, :], preferred_element_type=F32)
            o_ref[rows, cols] = (o / total).astype(BF16)


def shards(tokens_in, norm_gain, segment_ids, wq, wk, wv):
    vmem = pl.BlockSpec(memory_space=pltpu.VMEM)
    dma = pltpu.SemaphoreType.DMA
    freqs = 500000.0 ** (-(np.arange(HD) % 64) / 64.0)
    q, k, v = pl.pallas_call(
        front,
        name="front",
        out_shape=[
            jax.ShapeDtypeStruct((ROWS, 512), BF16),
            jax.ShapeDtypeStruct((BAND, HD), BF16),
            jax.ShapeDtypeStruct((BAND, HD), BF16),
        ],
        in_specs=[vmem] * 7,
        out_specs=[vmem] * 3,
        scratch_shapes=[
            pltpu.VMEM((NZ, 16, COLS), BF16),
            pltpu.VMEM((32, 256, COLS), BF16),
            pltpu.VMEM((NZ, ROWS, FEAT), BF16),
            pltpu.VMEM((NZ, 1, ROWS), F32),
            pltpu.VMEM((ROWS, COLS), F32),
            pltpu.VMEM((2, ROWS, HD), F32),
            pltpu.VMEM((2, BAND, HD), BF16),
            dma((NZ,)), dma((NZ,)),
            dma((NZ,)), dma((NZ,)),
            dma((15,)), dma((15,)),
            dma((16,)), dma((16,)),
            dma((2, CHUNKS * 16)), dma((2, CHUNKS * 16)),
            dma((2, CHUNKS * 5)), dma((2, CHUNKS * 5)),
        ],
        compiler_params=pltpu.CompilerParams(collective_id=1, has_side_effects=True, vmem_limit_bytes=48 << 20),
        cost_estimate=pl.CostEstimate(flops=2 * ROWS * 8192 * COLS, bytes_accessed=4 << 20, transcendentals=0),
    )(tokens_in, norm_gain[None], segment_ids, jnp.asarray(freqs[None], F32), wq, wk, wv)
    return pl.pallas_call(
        attend,
        name="attend",
        out_shape=jax.ShapeDtypeStruct((ROWS, 512), BF16),
        in_specs=[vmem] * 4,
        out_specs=vmem,
        scratch_shapes=[pltpu.VMEM((CHUNK, BACK * ROWS + CHUNK), F32)],
        compiler_params=pltpu.CompilerParams(vmem_limit_bytes=32 << 20),
        cost_estimate=pl.CostEstimate(flops=4 * 4 * ROWS * 1664 * HD, bytes_accessed=4 << 20, transcendentals=4 * ROWS * 1664),
    )(q, k, v, segment_ids)


def solution(mesh):
    placed = (
        P(("group", "fsdp"), "tensor"),
        P("tensor"),
        P("group", None),
        P(("group", "fsdp", "tensor"), None),
        P(("group", "fsdp", "tensor"), None),
        P(("group", "fsdp", "tensor"), None),
    )
    return jax.shard_map(
        shards,
        mesh=mesh,
        in_specs=placed,
        out_specs=P(("group", "fsdp"), "tensor"),
        check_vma=False,
    )
```

```python
import math

import jax
import jax.numpy as jnp
import numpy as np
from jax import lax
from jax.experimental import pallas as pl
from jax.experimental.pallas import tpu as pltpu
from jax.sharding import PartitionSpec as P

MESH = pl.DeviceIdType.MESH
F32, BF16 = jnp.float32, jnp.bfloat16
HD = 128
ROWS = 384
FEAT = 512
NZ = 16
SIZES = (192, 128, 64)
CHUNKS = len(SIZES)
FROM = (0, 192, 320)
LAG = 2
COLS = 768
BACK = 4
LOG2E = math.log2(math.e)
EPS = 1e-05


def document_starts(seg):
    return [jnp.sum(jnp.where(seg < d, 1.0, 0.0), axis=1, keepdims=True) for d in (1, 2, 3)]


def start_of(row, begins):
    start = jnp.zeros_like(row)
    for b in begins:
        start = jnp.where(row >= b, b, start)
    return start


def key_rows(ch, d):
    return pl.ds((BACK + 1) * FROM[ch] + (BACK - d) * SIZES[ch], SIZES[ch])


def front(tok_hbm, gain_ref, seg_hbm, freq_hbm, wq_hbm, wk_hbm, wv_hbm, o_ref,
          tok_ref, seg_ref, freq_ref, wq_ref, wk_ref, wv_ref,
          wsend, wbuf, tok, ssq, acc, trig, kv, queries, *rest):
    bias = rest[:CHUNKS]
    (peak, mixed, in_sem,
          a_send, a_recv, s_send, s_recv, p_send, p_recv, b_send, b_recv, r_send, r_recv, k_send, k_recv) = rest[CHUNKS:]
    g, f, z = lax.axis_index("group"), lax.axis_index("fsdp"), lax.axis_index("tensor")
    x, y, c = f // 2, (f % 2) * 2 + g // 2, g % 2

    def chip(px, py, core):
        return (py % 2) * 2 + core, px * 2 + py // 2

    def place(first, second, core=None):
        return chip((x + (1 - c) * first + c * second) % 4, (y + c * first + (1 - c) * second) % 4, c)

    def dev(gf, zz):
        return {"group": gf[0], "fsdp": gf[1], "tensor": zz}

    def copy(src, dst, send, recv, to):
        return pltpu.make_async_remote_copy(src_ref=src, dst_ref=dst, send_sem=send, recv_sem=recv, device_id=to, device_id_type=MESH)

    loads = [
        pltpu.make_async_copy(src, dst, in_sem.at[i])
        for i, (src, dst) in enumerate((
            (tok_hbm, tok_ref), (wq_hbm, wq_ref), (wk_hbm, wk_ref), (wv_hbm, wv_ref),
            (seg_hbm, seg_ref), (freq_hbm, freq_ref)))
    ]
    for load in loads:
        load.start()

    bar = pltpu.get_barrier_semaphore()
    count = 0
    for d in range(1, NZ):
        pl.semaphore_signal(bar, inc=1, device_id=dev((g, f), (z + d) % NZ), device_id_type=MESH)
        count += 1
    for d in (1, 3):
        for to in (place(d, 0), place(0, d)):
            pl.semaphore_signal(bar, inc=1, device_id=dev(to, z), device_id_type=MESH)
            count += 1
    sibling = chip(x, y, 1 - c)
    pl.semaphore_signal(bar, inc=1, device_id=dev(sibling, z), device_id_type=MESH)
    count += 1
    for d in range(1, 8):
        pl.semaphore_signal(bar, inc=1, device_id=dev((g, (f + d) % 8), z), device_id_type=MESH)
        count += 1

    loads[0].wait()
    floats = tok_ref[...].astype(F32)
    part = jnp.sum(floats * floats, axis=1, keepdims=True)
    ssq[z] = jnp.broadcast_to(part, (ROWS, 128)).T[0:1]

    for load in loads[1:4]:
        load.wait()
    for d in range(NZ):
        wsend[d, :, 0:512] = wq_ref[:, 512 * d:512 * d + 512].astype(BF16)
        head = slice(HD * (d // 2), HD * (d // 2) + HD)
        wsend[d, :, 512:640] = wk_ref[:, head].astype(BF16)
        wsend[d, :, 640:768] = wv_ref[:, head].astype(BF16)
    slot = g * 8 + f
    my_rows = pl.ds(pl.multiple_of(z * 16, 16), 16)

    pl.semaphore_wait(bar, count)

    def square(d):
        to = (z + d) % NZ
        return copy(ssq.at[z], ssq.at[z], s_send.at[d], s_recv.at[d], dev((g, f), to))

    def relay(d):
        to = (z + d) % NZ
        return copy(wsend.at[to], wbuf.at[slot, my_rows], a_send.at[d], a_recv.at[d], dev((g, f), to))

    for d in range(1, NZ):
        square(d).start()
    for d in range(1, NZ):
        relay(d).start()
    wbuf[slot, my_rows, :] = wsend[z]

    kv[:, 256:384] = jnp.ones(((BACK + 1) * ROWS, HD), BF16)
    for d in range(1, BACK + 1):
        @pl.when(f < d)
        def _():
            for ch in range(CHUNKS):
                kv[key_rows(ch, d), 0:256] = jnp.zeros((SIZES[ch], 256), BF16)

    for load in loads[4:]:
        load.wait()
    begins = document_starts(seg_ref[...])
    row = (lax.broadcasted_iota(jnp.int32, (ROWS, HD), 0) + f * ROWS).astype(F32)
    start = start_of(row, begins)
    angle = (row - start) * freq_ref[...]
    cosine, sine = jnp.cos(angle), jnp.sin(angle)
    lane = lax.broadcasted_iota(jnp.int32, (ROWS, HD), 1)
    trig[0] = cosine
    trig[1] = jnp.where(lane < HD // 2, -sine, sine)

    for d in range(1, NZ):
        square(d).wait_recv()
    total = jnp.sum(ssq[...], axis=0)
    scale = lax.rsqrt(jnp.broadcast_to(total, (128, ROWS)).T * (1.0 / 8192) + EPS)
    for j in range(FEAT // 128):
        cut = slice(128 * j, 128 * j + 128)
        tok[z, :, cut] = (tok_ref[:, cut].astype(F32) * scale * gain_ref[:, cut].astype(F32)).astype(BF16)

    def hop(ch, step, h, r):
        to = (z + 1 - 2 * r + NZ) % NZ
        owner = (z + NZ + (2 * r - 1) * step) % NZ
        ref = tok.at[owner, pl.ds(FROM[ch] + h * SIZES[ch] // 2, SIZES[ch] // 2)]
        i = (ch * 8 + step) * 2 + h
        return copy(ref, ref, r_send.at[r, i], r_recv.at[r, i], dev((g, f), to))

    WAYS = ((0, 0), (0, 1), (1, 0), (1, 1))

    def is_long(h, r):
        return h == r

    def ring(ch, step, h):
        for r in (0, 1):
            if step > 0:
                hop(ch, step - 1, h, r).wait_recv()
            if is_long(h, r) or step < 7:
                hop(ch, step, h, r).start()

    def last_arrivals(ch):
        for h in (0, 1):
            hop(ch, 7, h, h).wait_recv()

    def slot_at(first, second):
        gf = place(first, second)
        return gf[0] * 8 + gf[1]

    def ring4_ref(k, pos):
        return wbuf.at[slot_at(pos, 0) if k == 0 else slot_at(k - 1, pos)]

    def ring4_place(k, d):
        return place(d, 0) if k == 0 else place(0, d)

    def near(k, d):
        ref = ring4_ref(k, 0)
        i = k * 4 + d // 2
        return copy(ref, ref, p_send.at[i], p_recv.at[i], dev(ring4_place(k, d), z))

    def far(k, d):
        ref = ring4_ref(k, 4 - d).at[pl.ds((d // 2) * 128, 128)]
        i = k * 4 + 2 + d // 2
        return copy(ref, ref, p_send.at[i], p_recv.at[i], dev(ring4_place(k, d), z))

    def to_sibling(j, d):
        ref = wbuf.at[slot_at(j, d)]
        i = j * 4 + d
        return copy(ref, ref, b_send.at[i], b_recv.at[i], dev(sibling, z))

    def start_ring4(k):
        near(k, 1).start()
        near(k, 3).start()

    def forward_ring4(k):
        for d in (1, 3):
            near(k, d).wait_recv()
            far(k, d).start()

    def end_ring4(k):
        for d in (1, 3):
            far(k, d).wait_recv()

    def plane1():
        for d in range(1, NZ):
            relay(d).wait_recv()
        start_ring4(0)
        start_ring4(1)
        to_sibling(0, 0).start()

    def plane2():
        forward_ring4(0)
        start_ring4(4)
        start_ring4(2)
        to_sibling(3, 0).start()
        to_sibling(1, 0).start()

    def plane3():
        end_ring4(0)
        start_ring4(3)
        to_sibling(2, 0).start()
        forward_ring4(1)
        to_sibling(0, 3).start()
        to_sibling(0, 1).start()

    def plane4():
        for k in (4, 2):
            forward_ring4(k)
            to_sibling(k - 1, 3).start()
            to_sibling(k - 1, 1).start()
        end_ring4(1)
        to_sibling(0, 2).start()

    def plane5():
        forward_ring4(3)
        to_sibling(2, 3).start()
        to_sibling(2, 1).start()
        for k in (4, 2):
            end_ring4(k)
            to_sibling(k - 1, 2).start()

    def plane6():
        end_ring4(3)
        to_sibling(2, 2).start()
        for j in range(4):
            for d in range(4):
                to_sibling(j, d).wait_recv()

    def multiply(rows, low, high):
        def one(i, _):
            owner = (z + (i + 1) // 2 * (2 * (i % 2) - 1) + NZ) % NZ
            w = wbuf[pl.ds(owner * 2, 2)].reshape(FEAT, COLS)
            acc[rows, :] += jnp.dot(tok[owner, rows, :], w, preferred_element_type=F32)
            return 0

        if high - low == 1:
            one(low, 0)
        elif high > low:
            lax.fori_loop(low, high, one, 0)

    def kv_copy(ch, d):
        src, dst = (kv.at[key_rows(ch, back), pl.ds(0, 256)] for back in (0, d))
        i = ch * 4 + d - 1
        return copy(src, dst, k_send.at[i], k_recv.at[i], dev((g, (f + d) % 8), z))

    def finish(ch):
        size = SIZES[ch]
        rows = slice(FROM[ch], FROM[ch] + size)
        cosine, sine = trig[0, rows, :], trig[1, rows, :]
        for h in range(4):
            a = acc[rows, HD * h:HD * h + HD]
            queries[h, rows, :] = (a * cosine + pltpu.roll(a, HD // 2, 1) * sine).astype(BF16)
        a = acc[rows, 512:640]
        kv[key_rows(ch, 0), 0:128] = (a * cosine + pltpu.roll(a, HD // 2, 1) * sine).astype(BF16)
        kv[key_rows(ch, 0), 128:256] = acc[rows, 640:768].astype(BF16)
        for d in (4, 3, 2, 1):
            @pl.when(f + d < 8)
            def _():
                kv_copy(ch, d).start()

    def masks(ch):
        size = SIZES[ch]
        n = lax.broadcasted_iota(jnp.int32, (1, (BACK + 1) * size), 1)
        k_at = n + ((f - BACK) * ROWS + FROM[ch])
        for b in range(1, BACK + 1):
            k_at = k_at + jnp.where(n >= b * size, ROWS - size, 0)
        k_at = k_at.astype(F32)
        bias[ch][...] = jnp.where((k_at >= start[:, 0:1]) & (k_at <= row[:, 0:1]), 0.0, -1e30)

    def kv_arrivals(ch):
        for d in range(1, BACK + 1):
            @pl.when(f >= d)
            def _():
                kv_copy(ch, d).wait_recv()

    def attend(j, low, high, heads=range(4)):
        rows = slice(low, high)
        keys = slice((BACK + 1) * FROM[j], (BACK + 1) * (FROM[j] + SIZES[j]))
        for h in heads:
            s = lax.dot_general(queries[h, rows, :], kv[keys, 0:128], (((1,), (1,)), ((), ())), preferred_element_type=F32)
            s = s * (HD ** (-0.5) * LOG2E) + bias[j][rows, :]
            top = jnp.max(s, axis=1, keepdims=True)
            if j > 0:
                before = peak[h, rows, :]
                top = jnp.maximum(before[:, 0:1], top)
            p = jnp.exp2(s - top).astype(BF16)
            o = jnp.dot(p, kv[keys, 128:384], preferred_element_type=F32)
            if j > 0:
                keep = jnp.exp2(before - top)
                o = mixed[h, rows, :] * jnp.concatenate([keep, keep], axis=1) + o
            if j == CHUNKS - 1:
                o_ref[rows, HD * h:HD * h + HD] = (o[:, 0:128] / o[:, 128:256]).astype(BF16)
            else:
                peak[h, rows, :] = jnp.broadcast_to(top, (high - low, HD))
                mixed[h, rows, :] = o

    acc[...] = jnp.zeros((ROWS, COLS), F32)
    then = {
        (0, 0, 1): lambda: masks(0),
        (1, 0, 1): lambda: masks(1),
        (1, 1, 0): lambda: masks(2),
        (0, 2, 1): plane1,
        (2, 1, 1): plane2,
        (3, 1, 1): plane3,
        (4, 1, 1): plane4,
        (5, 1, 1): plane5,
        (6, 1, 1): plane6,
        (10, 1, 1): lambda: (kv_arrivals(0), attend(0, 0, FROM[2], (0, 1))),
        (11, 2, 0): lambda: attend(0, 0, FROM[2], (2,)),
        (11, 2, 1): lambda: attend(0, 0, FROM[2], (3,)),
    }
    weights_in = (6, 2, 0)
    done = [0] * CHUNKS
    have = [0] * CHUNKS
    ended = 0
    for t in range(8 + LAG * (CHUNKS - 1)):
        for ch in sorted(range(CHUNKS), key=lambda ch: t - LAG * ch >= 8):
            step = t - LAG * ch
            if step == 8:
                last_arrivals(ch)
                have[ch] = NZ
            for h in (0, 1):
                if 0 <= step < 8:
                    ring(ch, step, h)
                    if h == 1:
                        have[ch] = 2 * step + 1
                if (t, ch, h) >= weights_in and (0 <= step < 8 or step == 8 and h == 1):
                    for _ in range(2):
                        at = done[ended]
                        if all(done[k] == at and have[k] > at for k in range(ended, CHUNKS)):
                            multiply(slice(FROM[ended], ROWS), at, at + 1)
                            done[ended:] = [at + 1] * (CHUNKS - ended)
                if step == 8 and h == 1:
                    multiply(slice(FROM[ch], FROM[ch] + SIZES[ch]), done[ch], NZ)
                    finish(ch)
                    ended = ch + 1
                then.get((t, ch, h), lambda: None)()
    multiply(slice(FROM[2], ROWS), done[2], NZ - 1)
    last_arrivals(2)
    multiply(slice(FROM[2], ROWS), NZ - 1, NZ)
    finish(2)
    attend(0, FROM[2], ROWS)
    kv_arrivals(1)
    attend(1, 0, ROWS)
    kv_arrivals(2)
    attend(2, 0, ROWS)

    for d in range(1, NZ):
        square(d).wait_send()
        relay(d).wait_send()
    for k in range(5):
        for d in (1, 3):
            near(k, d).wait_send()
            far(k, d).wait_send()
    for j in range(4):
        for d in range(4):
            to_sibling(j, d).wait_send()

    for ch in range(CHUNKS):
        for step in range(8):
            for h, r in WAYS:
                if is_long(h, r) or step < 7:
                    hop(ch, step, h, r).wait_send()
    for ch in range(CHUNKS):
        for d in range(1, BACK + 1):
            @pl.when(f + d < 8)
            def _():
                kv_copy(ch, d).wait_send()


def shards(tokens_in, norm_gain, segment_ids, wq, wk, wv):
    vmem = pl.BlockSpec(memory_space=pltpu.VMEM)
    dma = pltpu.SemaphoreType.DMA
    freqs = 500000.0 ** (-(np.arange(HD) % 64) / 64.0)
    hbm = pl.BlockSpec(memory_space=pl.ANY)
    return pl.pallas_call(
        front,
        name="front",
        out_shape=jax.ShapeDtypeStruct((ROWS, 512), BF16),
        in_specs=[hbm, vmem] + [hbm] * 5,
        out_specs=vmem,
        scratch_shapes=[
            pltpu.VMEM((ROWS, FEAT), BF16),
            pltpu.VMEM((1, 8 * ROWS), jnp.int32),
            pltpu.VMEM((1, HD), F32),
            pltpu.VMEM((16, 8192), F32),
            pltpu.VMEM((16, 1024), F32),
            pltpu.VMEM((16, 1024), F32),
            pltpu.VMEM((NZ, 16, COLS), BF16),
            pltpu.VMEM((32, 256, COLS), BF16),
            pltpu.VMEM((NZ, ROWS, FEAT), BF16),
            pltpu.VMEM((NZ, 1, ROWS), F32),
            pltpu.VMEM((ROWS, COLS), F32),
            pltpu.VMEM((2, ROWS, HD), F32),
            pltpu.VMEM(((BACK + 1) * ROWS, 3 * HD), BF16),
            pltpu.VMEM((4, ROWS, HD), BF16),
            *[pltpu.VMEM((ROWS, (BACK + 1) * size), F32) for size in SIZES],
            pltpu.VMEM((4, ROWS, HD), F32),
            pltpu.VMEM((4, ROWS, 2 * HD), F32),
            dma((6,)),
            dma((NZ,)), dma((NZ,)),
            dma((NZ,)), dma((NZ,)),
            dma((20,)), dma((20,)),
            dma((16,)), dma((16,)),
            dma((2, CHUNKS * 16)), dma((2, CHUNKS * 16)),
            dma((CHUNKS * 4,)), dma((CHUNKS * 4,)),
        ],
        compiler_params=pltpu.CompilerParams(collective_id=1, has_side_effects=True, vmem_limit_bytes=56 << 20),
        cost_estimate=pl.CostEstimate(flops=2 * ROWS * 8192 * COLS, bytes_accessed=4 << 20, transcendentals=0),
    )(tokens_in, norm_gain[None], segment_ids, jnp.asarray(freqs[None], F32), wq, wk, wv)


def solution(mesh):
    placed = (
        P(("group", "fsdp"), "tensor"),
        P("tensor"),
        P("group", None),
        P(("group", "fsdp", "tensor"), None),
        P(("group", "fsdp", "tensor"), None),
        P(("group", "fsdp", "tensor"), None),
    )
    return jax.shard_map(
        shards,
        mesh=mesh,
        in_specs=placed,
        out_specs=P(("group", "fsdp"), "tensor"),
        check_vma=False,
    )
```

```python
import math

import jax
import jax.numpy as jnp
import numpy as np
from jax import lax
from jax.experimental import pallas as pl
from jax.experimental.pallas import tpu as pltpu
from jax.sharding import PartitionSpec as P

MESH = pl.DeviceIdType.MESH
F32, BF16 = jnp.float32, jnp.bfloat16
HD = 128
ROWS = 384
FEAT = 512
NZ = 16
SIZES = (192, 128, 64)
CHUNKS = len(SIZES)
FROM = (0, 192, 320)
START = (0, 2, 3)
COLS = 768
BACK = 4
RELAYED = (0,)
LOG2E = math.log2(math.e)
EPS = 1e-05


def document_starts(seg):
    return [jnp.sum(jnp.where(seg < d, 1.0, 0.0), axis=1, keepdims=True) for d in (1, 2, 3)]


def start_of(row, begins):
    start = jnp.zeros_like(row)
    for b in begins:
        start = jnp.where(row >= b, b, start)
    return start


def key_rows(ch, d):
    return pl.ds((BACK + 1) * FROM[ch] + (BACK - d) * SIZES[ch], SIZES[ch])


def front(tok_hbm, gain_ref, seg_hbm, freq_hbm, wq_hbm, wk_hbm, wv_hbm, o_ref,
          tok_ref, seg_ref, freq_ref, wq_ref, wk_ref, wv_ref,
          wsend, wbuf, tok, ssq, acc, trig, kv, queries, *rest):
    bias = rest[:CHUNKS]
    (peak, mixed, in_sem,
          a_send, a_recv, s_send, s_recv, p_send, p_recv, b_send, b_recv, r_send, r_recv, k_send, k_recv, r_kv_send) = rest[CHUNKS:]
    g, f, z = lax.axis_index("group"), lax.axis_index("fsdp"), lax.axis_index("tensor")
    x, y, c = f // 2, (f % 2) * 2 + g // 2, g % 2

    def chip(px, py, core):
        return (py % 2) * 2 + core, px * 2 + py // 2

    def place(first, second, core=None):
        return chip((x + (1 - c) * first + c * second) % 4, (y + c * first + (1 - c) * second) % 4, c)

    def dev(gf, zz):
        return {"group": gf[0], "fsdp": gf[1], "tensor": zz}

    def copy(src, dst, send, recv, to):
        return pltpu.make_async_remote_copy(src_ref=src, dst_ref=dst, send_sem=send, recv_sem=recv, device_id=to, device_id_type=MESH)

    loads = [
        pltpu.make_async_copy(src, dst, in_sem.at[i])
        for i, (src, dst) in enumerate((
            (tok_hbm, tok_ref), (wq_hbm, wq_ref), (wk_hbm, wk_ref), (wv_hbm, wv_ref),
            (seg_hbm, seg_ref), (freq_hbm, freq_ref)))
    ]
    bar = pltpu.get_barrier_semaphore()
    count = 0
    for d in range(1, NZ):
        pl.semaphore_signal(bar, inc=1, device_id=dev((g, f), (z + d) % NZ), device_id_type=MESH)
        count += 1
    for d in (1, 3):
        for to in (place(d, 0), place(0, d)):
            pl.semaphore_signal(bar, inc=1, device_id=dev(to, z), device_id_type=MESH)
            count += 1
    sibling = chip(x, y, 1 - c)
    pl.semaphore_signal(bar, inc=1, device_id=dev(sibling, z), device_id_type=MESH)
    count += 1
    for d in range(1, 8):
        pl.semaphore_signal(bar, inc=1, device_id=dev((g, (f + d) % 8), z), device_id_type=MESH)
        count += 1

    for load in loads:
        load.start()

    loads[0].wait()
    floats = tok_ref[...].astype(F32)
    part = jnp.sum(floats * floats, axis=1, keepdims=True)
    ssq[z] = jnp.broadcast_to(part, (ROWS, 128)).T[0:1]

    for load in loads[1:4]:
        load.wait()
    for d in range(NZ):
        wsend[d, :, 0:512] = wq_ref[:, 512 * d:512 * d + 512].astype(BF16)
        head = slice(HD * (d // 2), HD * (d // 2) + HD)
        wsend[d, :, 512:640] = wk_ref[:, head].astype(BF16)
        wsend[d, :, 640:768] = wv_ref[:, head].astype(BF16)
    slot = g * 8 + f
    my_rows = pl.ds(pl.multiple_of(z * 16, 16), 16)

    pl.semaphore_wait(bar, count)

    def square(d):
        to = (z + d) % NZ
        return copy(ssq.at[z], ssq.at[z], s_send.at[d], s_recv.at[d], dev((g, f), to))

    def relay(d):
        to = (z + d) % NZ
        return copy(wsend.at[to], wbuf.at[slot, my_rows], a_send.at[d], a_recv.at[d], dev((g, f), to))

    for d in range(1, NZ):
        square(d).start()
    for d in range(1, NZ):
        relay(d).start()
    wbuf[slot, my_rows, :] = wsend[z]

    kv[:, 256:384] = jnp.ones(((BACK + 1) * ROWS, HD), BF16)
    for d in range(1, BACK + 1):
        @pl.when(f < d)
        def _():
            for ch in range(CHUNKS):
                kv[key_rows(ch, d), 0:256] = jnp.zeros((SIZES[ch], 256), BF16)

    for load in loads[4:]:
        load.wait()
    begins = document_starts(seg_ref[...])
    row = (lax.broadcasted_iota(jnp.int32, (ROWS, HD), 0) + f * ROWS).astype(F32)
    start = start_of(row, begins)
    angle = (row - start) * freq_ref[...]
    cosine, sine = jnp.cos(angle), jnp.sin(angle)
    lane = lax.broadcasted_iota(jnp.int32, (ROWS, HD), 1)
    trig[0] = cosine
    trig[1] = jnp.where(lane < HD // 2, -sine, sine)

    for d in range(1, NZ):
        square(d).wait_recv()
    total = jnp.sum(ssq[...], axis=0)
    scale = lax.rsqrt(jnp.broadcast_to(total, (128, ROWS)).T * (1.0 / 8192) + EPS)
    for j in range(FEAT // 128):
        cut = slice(128 * j, 128 * j + 128)
        tok[z, :, cut] = (tok_ref[:, cut].astype(F32) * scale * gain_ref[cut].astype(F32)[None]).astype(BF16)

    def hop(ch, step, h, r):
        to = (z + 1 - 2 * r + NZ) % NZ
        owner = (z + NZ + (2 * r - 1) * step) % NZ
        ref = tok.at[owner, pl.ds(FROM[ch] + h * SIZES[ch] // 2, SIZES[ch] // 2)]
        i = (ch * 8 + step) * 2 + h
        return copy(ref, ref, r_send.at[r, i], r_recv.at[r, i], dev((g, f), to))

    WAYS = ((0, 0), (0, 1), (1, 0), (1, 1))

    def is_long(h, r):
        return h == r

    def ring(ch, step, h):
        for r in (0, 1):
            if step > 0:
                hop(ch, step - 1, h, r).wait_recv()
            if is_long(h, r) or step < 7:
                hop(ch, step, h, r).start()

    def last_arrivals(ch):
        for h in (0, 1):
            hop(ch, 7, h, h).wait_recv()

    def slot_at(first, second):
        gf = place(first, second)
        return gf[0] * 8 + gf[1]

    def ring4_ref(k, pos):
        return wbuf.at[slot_at(pos, 0) if k == 0 else slot_at(k - 1, pos)]

    def ring4_place(k, d):
        return place(d, 0) if k == 0 else place(0, d)

    def near(k, d):
        ref = ring4_ref(k, 0)
        i = k * 4 + d // 2
        return copy(ref, ref, p_send.at[i], p_recv.at[i], dev(ring4_place(k, d), z))

    def far(k, d):
        ref = ring4_ref(k, 4 - d).at[pl.ds((d // 2) * 128, 128)]
        i = k * 4 + 2 + d // 2
        return copy(ref, ref, p_send.at[i], p_recv.at[i], dev(ring4_place(k, d), z))

    def to_sibling(j, d):
        ref = wbuf.at[slot_at(j, d)]
        i = j * 4 + d
        return copy(ref, ref, b_send.at[i], b_recv.at[i], dev(sibling, z))

    def start_ring4(k):
        near(k, 1).start()
        near(k, 3).start()

    def forward_ring4(k):
        for d in (1, 3):
            near(k, d).wait_recv()
            far(k, d).start()

    def end_ring4(k):
        for d in (1, 3):
            far(k, d).wait_recv()

    def plane1():
        for d in range(1, NZ):
            relay(d).wait_recv()
        start_ring4(0)
        start_ring4(1)
        to_sibling(0, 0).start()

    def plane2():
        forward_ring4(0)
        start_ring4(4)
        start_ring4(2)
        to_sibling(3, 0).start()
        to_sibling(1, 0).start()

    def plane3():
        end_ring4(0)
        start_ring4(3)
        to_sibling(2, 0).start()
        forward_ring4(1)
        to_sibling(0, 3).start()
        to_sibling(0, 1).start()

    def plane4():
        for k in (4, 2):
            forward_ring4(k)
            to_sibling(k - 1, 3).start()
            to_sibling(k - 1, 1).start()
        end_ring4(1)
        to_sibling(0, 2).start()

    def plane5():
        forward_ring4(3)
        to_sibling(2, 3).start()
        to_sibling(2, 1).start()
        for k in (4, 2):
            end_ring4(k)
            to_sibling(k - 1, 2).start()

    def plane6():
        end_ring4(3)
        to_sibling(2, 2).start()
        for j in range(4):
            for d in range(4):
                to_sibling(j, d).wait_recv()

    def multiply(rows, low, high):
        def one(i, _):
            owner = (z + (i + 1) // 2 * (2 * (i % 2) - 1) + NZ) % NZ
            w = wbuf[pl.ds(owner * 2, 2)].reshape(FEAT, COLS)
            acc[rows, :] += jnp.dot(tok[owner, rows, :], w, preferred_element_type=F32)
            return 0

        if high - low == 1:
            one(low, 0)
        elif high > low:
            lax.fori_loop(low, high, one, 0)

    def kv_copy(ch, d):
        src, dst = (kv.at[key_rows(ch, back), pl.ds(0, 256)] for back in (0, d))
        i = ch * 4 + d - 1
        return copy(src, dst, k_send.at[i], k_recv.at[i], dev((g, (f + d) % 8), z))

    def kv_relay(ch, d):
        at = d + 1 - 2 * (f % 2)
        src = kv.at[key_rows(ch, d), pl.ds(0, 256)]
        dst = kv.at[pl.ds(pl.multiple_of((BACK + 1) * FROM[ch] + (BACK - at) * SIZES[ch], 32), SIZES[ch]), pl.ds(0, 256)]
        return copy(src, dst, r_kv_send.at[ch * 2 + d // 2 - 1], k_recv.at[ch * 4 + at - 1], dev((g, f + 1 - 2 * (f % 2)), z))

    def relays(ch, d):
        @pl.when((f >= d) & (f % 2 >= d // 4))
        def _():
            kv_copy(ch, d).wait_recv()
            kv_relay(ch, d).start()

    def finish(ch):
        size = SIZES[ch]
        rows = slice(FROM[ch], FROM[ch] + size)
        cosine, sine = trig[0, rows, :], trig[1, rows, :]
        for h in range(4):
            a = acc[rows, HD * h:HD * h + HD]
            queries[h, rows, :] = (a * cosine + pltpu.roll(a, HD // 2, 1) * sine).astype(BF16)
        a = acc[rows, 512:640]
        kv[key_rows(ch, 0), 0:128] = (a * cosine + pltpu.roll(a, HD // 2, 1) * sine).astype(BF16)
        kv[key_rows(ch, 0), 128:256] = acc[rows, 640:768].astype(BF16)
        if ch in RELAYED:
            for d in (4, 2):
                @pl.when(f + d < 8)
                def _():
                    kv_copy(ch, d).start()

            @pl.when(f % 2 == 0)
            def _():
                kv_copy(ch, 1).start()
        else:
            for d in (4, 3, 2, 1):
                @pl.when(f + d < 8)
                def _():
                    kv_copy(ch, d).start()

    def masks(ch):
        size = SIZES[ch]
        n = lax.broadcasted_iota(jnp.int32, (1, (BACK + 1) * size), 1)
        k_at = n + ((f - BACK) * ROWS + FROM[ch])
        for b in range(1, BACK + 1):
            k_at = k_at + jnp.where(n >= b * size, ROWS - size, 0)
        k_at = k_at.astype(F32)
        bias[ch][...] = jnp.where((k_at >= start[:, 0:1]) & (k_at <= row[:, 0:1]), 0.0, -1e30)

    def kv_arrivals(ch):
        for d in range(1, BACK + 1):
            taken = {2: 0, 4: 1}.get(d, 2) if ch in RELAYED else 2

            @pl.when((f >= d) & (f % 2 < taken))
            def _():
                kv_copy(ch, d).wait_recv()

    def attend(j, low, high, heads=range(4)):
        rows = slice(low, high)
        keys = slice((BACK + 1) * FROM[j], (BACK + 1) * (FROM[j] + SIZES[j]))
        for h in heads:
            s = lax.dot_general(queries[h, rows, :], kv[keys, 0:128], (((1,), (1,)), ((), ())), preferred_element_type=F32)
            s = s * (HD ** (-0.5) * LOG2E) + bias[j][rows, :]
            top = jnp.max(s, axis=1, keepdims=True)
            if j > 0:
                before = peak[h, rows, :]
                top = jnp.maximum(before[:, 0:1], top)
            p = jnp.exp2(s - top).astype(BF16)
            o = jnp.dot(p, kv[keys, 128:384], preferred_element_type=F32)
            if j > 0:
                keep = jnp.exp2(before - top)
                o = mixed[h, rows, :] * jnp.concatenate([keep, keep], axis=1) + o
            if j == CHUNKS - 1:
                o_ref[rows, HD * h:HD * h + HD] = (o[:, 0:128] / o[:, 128:256]).astype(BF16)
            else:
                peak[h, rows, :] = jnp.broadcast_to(top, (high - low, HD))
                mixed[h, rows, :] = o

    acc[...] = jnp.zeros((ROWS, COLS), F32)
    then = {
        (0, 0, 1): lambda: masks(0),
        (1, 0, 1): lambda: masks(1),
        (1, 1, 0): lambda: masks(2),
        (0, 2, 1): plane1,
        (2, 1, 1): plane2,
        (3, 1, 1): plane3,
        (4, 1, 1): plane4,
        (5, 1, 1): plane5,
        (6, 1, 1): plane6,
        (9, 2, 1): lambda: relays(0, 2),
        (10, 1, 1): lambda: relays(0, 4),
    }
    weights_in = (6, 2, 0)
    done = [0] * CHUNKS
    have = [0] * CHUNKS
    ended = 0
    for t in range(8 + START[-1]):
        for ch in sorted(range(CHUNKS), key=lambda ch: t - START[ch] >= 8):
            step = t - START[ch]
            if step == 8:
                last_arrivals(ch)
                have[ch] = NZ
            for h in (0, 1):
                if 0 <= step < 8:
                    ring(ch, step, h)
                    if h == 1:
                        have[ch] = 2 * step + 1
                if (t, ch, h) >= weights_in and (0 <= step < 8 or step == 8 and h == 1):
                    for _ in range(2):
                        at = done[ended]
                        if all(done[k] == at and have[k] > at for k in range(ended, CHUNKS)):
                            multiply(slice(FROM[ended], ROWS), at, at + 1)
                            done[ended:] = [at + 1] * (CHUNKS - ended)
                if step == 8 and h == 1:
                    multiply(slice(FROM[ch], FROM[ch] + SIZES[ch]), done[ch], NZ)
                    finish(ch)
                    ended = ch + 1
                then.get((t, ch, h), lambda: None)()
    multiply(slice(FROM[2], ROWS), done[2], NZ - 1)
    last_arrivals(2)
    multiply(slice(FROM[2], ROWS), NZ - 1, NZ)
    finish(2)
    kv_arrivals(0)
    attend(0, 0, ROWS)
    kv_arrivals(1)
    attend(1, 0, ROWS)
    kv_arrivals(2)
    attend(2, 0, ROWS)

    for d in range(1, NZ):
        square(d).wait_send()
        relay(d).wait_send()
    for k in range(5):
        for d in (1, 3):
            near(k, d).wait_send()
            far(k, d).wait_send()
    for j in range(4):
        for d in range(4):
            to_sibling(j, d).wait_send()

    for ch in range(CHUNKS):
        for step in range(8):
            for h, r in WAYS:
                if is_long(h, r) or step < 7:
                    hop(ch, step, h, r).wait_send()
    for ch in range(CHUNKS):
        if ch in RELAYED:
            for d in (2, 4):
                @pl.when(f + d < 8)
                def _():
                    kv_copy(ch, d).wait_send()

                @pl.when((f >= d) & (f % 2 >= d // 4))
                def _():
                    kv_relay(ch, d).wait_send()

            @pl.when(f % 2 == 0)
            def _():
                kv_copy(ch, 1).wait_send()
        else:
            for d in range(1, BACK + 1):
                @pl.when(f + d < 8)
                def _():
                    kv_copy(ch, d).wait_send()


def hand_over(in_ref, out_ref):
    out_ref[...] = in_ref[...]


def shards(tokens_in, norm_gain, segment_ids, wq, wk, wv):
    vmem = pl.BlockSpec(memory_space=pltpu.VMEM)
    dma = pltpu.SemaphoreType.DMA
    freqs = 500000.0 ** (-(np.arange(HD) % 64) / 64.0)
    hbm = pl.BlockSpec(memory_space=pl.ANY)
    attended = pl.pallas_call(
        front,
        name="front",
        out_shape=jax.ShapeDtypeStruct((ROWS, 512), BF16),
        in_specs=[hbm, vmem] + [hbm] * 5,
        out_specs=vmem,
        scratch_shapes=[
            pltpu.VMEM((ROWS, FEAT), BF16),
            pltpu.VMEM((1, 8 * ROWS), jnp.int32),
            pltpu.VMEM((1, HD), F32),
            pltpu.VMEM((16, 8192), F32),
            pltpu.VMEM((16, 1024), F32),
            pltpu.VMEM((16, 1024), F32),
            pltpu.VMEM((NZ, 16, COLS), BF16),
            pltpu.VMEM((32, 256, COLS), BF16),
            pltpu.VMEM((NZ, ROWS, FEAT), BF16),
            pltpu.VMEM((NZ, 1, ROWS), F32),
            pltpu.VMEM((ROWS, COLS), F32),
            pltpu.VMEM((2, ROWS, HD), F32),
            pltpu.VMEM(((BACK + 1) * ROWS, 3 * HD), BF16),
            pltpu.VMEM((4, ROWS, HD), BF16),
            *[pltpu.VMEM((ROWS, (BACK + 1) * size), F32) for size in SIZES],
            pltpu.VMEM((4, ROWS, HD), F32),
            pltpu.VMEM((4, ROWS, 2 * HD), F32),
            dma((6,)),
            dma((NZ,)), dma((NZ,)),
            dma((NZ,)), dma((NZ,)),
            dma((20,)), dma((20,)),
            dma((16,)), dma((16,)),
            dma((2, CHUNKS * 16)), dma((2, CHUNKS * 16)),
            dma((CHUNKS * 4,)), dma((CHUNKS * 4,)), dma((CHUNKS * 2,)),
        ],
        compiler_params=pltpu.CompilerParams(collective_id=1, has_side_effects=True, vmem_limit_bytes=56 << 20),
        cost_estimate=pl.CostEstimate(flops=2 * ROWS * 8192 * COLS, bytes_accessed=4 << 20, transcendentals=0),
    )(tokens_in, norm_gain, segment_ids, jnp.asarray(freqs[None], F32), wq, wk, wv)
    return pl.pallas_call(
        hand_over,
        name="hand_over",
        out_shape=jax.ShapeDtypeStruct((ROWS, 512), BF16),
        in_specs=[vmem],
        out_specs=vmem,
    )(attended)


def solution(mesh):
    placed = (
        P(("group", "fsdp"), "tensor"),
        P("tensor"),
        P("group", None),
        P(("group", "fsdp", "tensor"), None),
        P(("group", "fsdp", "tensor"), None),
        P(("group", "fsdp", "tensor"), None),
    )
    return jax.shard_map(
        shards,
        mesh=mesh,
        in_specs=placed,
        out_specs=P(("group", "fsdp"), "tensor"),
        check_vma=False,
    )
```

```python
import math

import jax
import jax.numpy as jnp
import numpy as np
from jax import lax
from jax.experimental import pallas as pl
from jax.experimental.pallas import tpu as pltpu
from jax.sharding import PartitionSpec as P

MESH = pl.DeviceIdType.MESH
F32, BF16 = jnp.float32, jnp.bfloat16
HD = 128
ROWS = 384
FEAT = 512
NZ = 16
SIZES = (192, 128, 64)
CHUNKS = len(SIZES)
FROM = (0, 192, 320)
START = (0, 2, 3)
COLS = 768
BACK = 4
RELAYED = (0,)
LOG2E = math.log2(math.e)
EPS = 1e-05


def document_starts(seg):
    return [jnp.sum(jnp.where(seg < d, 1.0, 0.0), axis=1, keepdims=True) for d in (1, 2, 3)]


def start_of(row, begins):
    start = jnp.zeros_like(row)
    for b in begins:
        start = jnp.where(row >= b, b, start)
    return start


def key_rows(ch, d):
    return pl.ds((BACK + 1) * FROM[ch] + (BACK - d) * SIZES[ch], SIZES[ch])


def front(tok_hbm, gain_ref, seg_hbm, freq_hbm, wq_hbm, wk_hbm, wv_hbm, o_ref,
          tok_ref, seg_ref, freq_ref, wq_ref, wk_ref, wv_ref,
          wsend, wbuf, tok, ssq, acc, trig, kv, queries, *rest):
    bias = rest[:CHUNKS]
    (peak, mixed, in_sem,
          a_send, a_recv, s_send, s_recv, p_send, p_recv, b_send, b_recv, r_send, r_recv, k_send, k_recv, r_kv_send) = rest[CHUNKS:]
    g, f, z = lax.axis_index("group"), lax.axis_index("fsdp"), lax.axis_index("tensor")
    x, y, c = f // 2, (f % 2) * 2 + g // 2, g % 2

    def chip(px, py, core):
        return (py % 2) * 2 + core, px * 2 + py // 2

    def place(first, second, core=None):
        return chip((x + (1 - c) * first + c * second) % 4, (y + c * first + (1 - c) * second) % 4, c)

    def dev(gf, zz):
        return {"group": gf[0], "fsdp": gf[1], "tensor": zz}

    def copy(src, dst, send, recv, to):
        return pltpu.make_async_remote_copy(src_ref=src, dst_ref=dst, send_sem=send, recv_sem=recv, device_id=to, device_id_type=MESH)

    loads = [
        pltpu.make_async_copy(src, dst, in_sem.at[i])
        for i, (src, dst) in enumerate((
            (tok_hbm, tok_ref), (wq_hbm, wq_ref), (wk_hbm, wk_ref), (wv_hbm, wv_ref),
            (seg_hbm, seg_ref), (freq_hbm, freq_ref)))
    ]
    bar = pltpu.get_barrier_semaphore()
    count = 0
    for d in range(1, NZ):
        pl.semaphore_signal(bar, inc=1, device_id=dev((g, f), (z + d) % NZ), device_id_type=MESH)
        count += 1
    for d in (1, 3):
        for to in (place(d, 0), place(0, d)):
            pl.semaphore_signal(bar, inc=1, device_id=dev(to, z), device_id_type=MESH)
            count += 1
    sibling = chip(x, y, 1 - c)
    pl.semaphore_signal(bar, inc=1, device_id=dev(sibling, z), device_id_type=MESH)
    count += 1
    for d in range(1, 8):
        pl.semaphore_signal(bar, inc=1, device_id=dev((g, (f + d) % 8), z), device_id_type=MESH)
        count += 1

    for load in loads:
        load.start()

    loads[0].wait()
    floats = tok_ref[...].astype(F32)
    part = jnp.sum(floats * floats, axis=1, keepdims=True)
    ssq[z] = jnp.broadcast_to(part, (ROWS, 128)).T[0:1]

    for load in loads[1:4]:
        load.wait()
    for d in range(NZ):
        wsend[d, :, 0:512] = wq_ref[:, 512 * d:512 * d + 512].astype(BF16)
        head = slice(HD * (d // 2), HD * (d // 2) + HD)
        wsend[d, :, 512:640] = wk_ref[:, head].astype(BF16)
        wsend[d, :, 640:768] = wv_ref[:, head].astype(BF16)
    slot = g * 8 + f
    my_rows = pl.ds(pl.multiple_of(z * 16, 16), 16)

    pl.semaphore_wait(bar, count)

    def square(d):
        to = (z + d) % NZ
        return copy(ssq.at[z], ssq.at[z], s_send.at[d], s_recv.at[d], dev((g, f), to))

    def relay(d):
        to = (z + d) % NZ
        return copy(wsend.at[to], wbuf.at[slot, my_rows], a_send.at[d], a_recv.at[d], dev((g, f), to))

    for d in range(1, NZ):
        square(d).start()
    for d in range(1, NZ):
        relay(d).start()
    wbuf[slot, my_rows, :] = wsend[z]

    kv[:, 256:384] = jnp.ones(((BACK + 1) * ROWS, HD), BF16)
    for d in range(1, BACK + 1):
        @pl.when(f < d)
        def _():
            for ch in range(CHUNKS):
                kv[key_rows(ch, d), 0:256] = jnp.zeros((SIZES[ch], 256), BF16)

    for load in loads[4:]:
        load.wait()
    begins = document_starts(seg_ref[...])
    row = (lax.broadcasted_iota(jnp.int32, (ROWS, HD), 0) + f * ROWS).astype(F32)
    start = start_of(row, begins)
    angle = (row - start) * freq_ref[...]
    cosine, sine = jnp.cos(angle), jnp.sin(angle)
    lane = lax.broadcasted_iota(jnp.int32, (ROWS, HD), 1)
    trig[0] = cosine
    trig[1] = jnp.where(lane < HD // 2, -sine, sine)

    for d in range(1, NZ):
        square(d).wait_recv()
    total = jnp.sum(ssq[...], axis=0)
    scale = lax.rsqrt(jnp.broadcast_to(total, (128, ROWS)).T * (1.0 / 8192) + EPS)
    for j in range(FEAT // 128):
        cut = slice(128 * j, 128 * j + 128)
        tok[z, :, cut] = (tok_ref[:, cut].astype(F32) * scale * gain_ref[cut].astype(F32)[None]).astype(BF16)

    def hop(ch, step, h, r):
        to = (z + 1 - 2 * r + NZ) % NZ
        owner = (z + NZ + (2 * r - 1) * step) % NZ
        ref = tok.at[owner, pl.ds(FROM[ch] + h * SIZES[ch] // 2, SIZES[ch] // 2)]
        i = (ch * 8 + step) * 2 + h
        return copy(ref, ref, r_send.at[r, i], r_recv.at[r, i], dev((g, f), to))

    WAYS = ((0, 0), (0, 1), (1, 0), (1, 1))

    def is_long(h, r):
        return h == r

    def ring(ch, step, h):
        for r in (0, 1):
            if step > 0:
                hop(ch, step - 1, h, r).wait_recv()
            if is_long(h, r) or step < 7:
                hop(ch, step, h, r).start()

    def last_arrivals(ch):
        for h in (0, 1):
            hop(ch, 7, h, h).wait_recv()

    def slot_at(first, second):
        gf = place(first, second)
        return gf[0] * 8 + gf[1]

    def ring4_ref(k, pos):
        return wbuf.at[slot_at(pos, 0) if k == 0 else slot_at(k - 1, pos)]

    def ring4_place(k, d):
        return place(d, 0) if k == 0 else place(0, d)

    def near(k, d):
        ref = ring4_ref(k, 0)
        i = k * 4 + d // 2
        return copy(ref, ref, p_send.at[i], p_recv.at[i], dev(ring4_place(k, d), z))

    def far(k, d):
        ref = ring4_ref(k, 4 - d).at[pl.ds((d // 2) * 128, 128)]
        i = k * 4 + 2 + d // 2
        return copy(ref, ref, p_send.at[i], p_recv.at[i], dev(ring4_place(k, d), z))

    def to_sibling(j, d):
        ref = wbuf.at[slot_at(j, d)]
        i = j * 4 + d
        return copy(ref, ref, b_send.at[i], b_recv.at[i], dev(sibling, z))

    def start_ring4(k):
        near(k, 1).start()
        near(k, 3).start()

    def forward_ring4(k):
        for d in (1, 3):
            near(k, d).wait_recv()
            far(k, d).start()

    def end_ring4(k):
        for d in (1, 3):
            far(k, d).wait_recv()

    def plane1():
        for d in range(1, NZ):
            relay(d).wait_recv()
        start_ring4(0)
        start_ring4(1)
        to_sibling(0, 0).start()

    def plane2():
        forward_ring4(0)
        start_ring4(4)
        start_ring4(2)
        to_sibling(3, 0).start()
        to_sibling(1, 0).start()

    def plane3():
        end_ring4(0)
        start_ring4(3)
        to_sibling(2, 0).start()
        forward_ring4(1)
        to_sibling(0, 3).start()
        to_sibling(0, 1).start()

    def plane4():
        for k in (4, 2):
            forward_ring4(k)
            to_sibling(k - 1, 3).start()
            to_sibling(k - 1, 1).start()
        end_ring4(1)
        to_sibling(0, 2).start()

    def plane5():
        forward_ring4(3)
        to_sibling(2, 3).start()
        to_sibling(2, 1).start()
        for k in (4, 2):
            end_ring4(k)
            to_sibling(k - 1, 2).start()

    def plane6():
        end_ring4(3)
        to_sibling(2, 2).start()
        for j in range(4):
            for d in range(4):
                to_sibling(j, d).wait_recv()

    def multiply(rows, low, high):
        def one(i, _):
            owner = (z + (i + 1) // 2 * (2 * (i % 2) - 1) + NZ) % NZ
            w = wbuf[pl.ds(owner * 2, 2)].reshape(FEAT, COLS)
            acc[rows, :] += jnp.dot(tok[owner, rows, :], w, preferred_element_type=F32)
            return 0

        if high - low == 1:
            one(low, 0)
        elif high > low:
            lax.fori_loop(low, high, one, 0)

    def kv_copy(ch, d):
        src, dst = (kv.at[key_rows(ch, back), pl.ds(0, 256)] for back in (0, d))
        i = ch * 4 + d - 1
        return copy(src, dst, k_send.at[i], k_recv.at[i], dev((g, (f + d) % 8), z))

    def kv_relay(ch, d):
        at = d + 1 - 2 * (f % 2)
        src = kv.at[key_rows(ch, d), pl.ds(0, 256)]
        dst = kv.at[pl.ds(pl.multiple_of((BACK + 1) * FROM[ch] + (BACK - at) * SIZES[ch], 32), SIZES[ch]), pl.ds(0, 256)]
        return copy(src, dst, r_kv_send.at[ch * 2 + d // 2 - 1], k_recv.at[ch * 4 + at - 1], dev((g, f + 1 - 2 * (f % 2)), z))

    def relays(ch, d):
        @pl.when((f >= d) & (f % 2 >= d // 4))
        def _():
            kv_copy(ch, d).wait_recv()
            kv_relay(ch, d).start()

    def finish(ch):
        size = SIZES[ch]
        rows = slice(FROM[ch], FROM[ch] + size)
        cosine, sine = trig[0, rows, :], trig[1, rows, :]
        for h in range(4):
            a = acc[rows, HD * h:HD * h + HD]
            queries[h, rows, :] = (a * cosine + pltpu.roll(a, HD // 2, 1) * sine).astype(BF16)
        a = acc[rows, 512:640]
        kv[key_rows(ch, 0), 0:128] = (a * cosine + pltpu.roll(a, HD // 2, 1) * sine).astype(BF16)
        kv[key_rows(ch, 0), 128:256] = acc[rows, 640:768].astype(BF16)
        if ch in RELAYED:
            for d in (4, 2):
                @pl.when(f + d < 8)
                def _():
                    kv_copy(ch, d).start()

            @pl.when(f % 2 == 0)
            def _():
                kv_copy(ch, 1).start()
        else:
            for d in (4, 3, 2, 1):
                @pl.when(f + d < 8)
                def _():
                    kv_copy(ch, d).start()

    def masks(ch):
        size = SIZES[ch]
        n = lax.broadcasted_iota(jnp.int32, (1, (BACK + 1) * size), 1)
        k_at = n + ((f - BACK) * ROWS + FROM[ch])
        for b in range(1, BACK + 1):
            k_at = k_at + jnp.where(n >= b * size, ROWS - size, 0)
        k_at = k_at.astype(F32)
        bias[ch][...] = jnp.where((k_at >= start[:, 0:1]) & (k_at <= row[:, 0:1]), 0.0, -1e30)

    def kv_arrivals(ch):
        for d in range(1, BACK + 1):
            taken = {2: 0, 4: 1}.get(d, 2) if ch in RELAYED else 2

            @pl.when((f >= d) & (f % 2 < taken))
            def _():
                kv_copy(ch, d).wait_recv()

    def attend(j, low, high, heads=range(4), skip=0):
        rows = slice(low, high)
        width = (BACK + 1) * SIZES[j] - skip
        keys = slice((BACK + 1) * FROM[j], (BACK + 1) * FROM[j] + width)
        for h in heads:
            s = lax.dot_general(queries[h, rows, :], kv[keys, 0:128], (((1,), (1,)), ((), ())), preferred_element_type=F32)
            s = s * (HD ** (-0.5) * LOG2E) + bias[j][rows, 0:width]
            top = jnp.max(s, axis=1, keepdims=True)
            if j > 0:
                before = peak[h, rows, :]
                top = jnp.maximum(before[:, 0:1], top)
            p = jnp.exp2(s - top).astype(BF16)
            o = jnp.dot(p, kv[keys, 128:384], preferred_element_type=F32)
            if j > 0:
                keep = jnp.exp2(before - top)
                o = mixed[h, rows, :] * jnp.concatenate([keep, keep], axis=1) + o
            if j == CHUNKS - 1:
                o_ref[rows, HD * h:HD * h + HD] = (o[:, 0:128] / o[:, 128:256]).astype(BF16)
            else:
                peak[h, rows, :] = jnp.broadcast_to(top, (high - low, HD))
                mixed[h, rows, :] = o

    acc[...] = jnp.zeros((ROWS, COLS), F32)
    then = {
        (0, 0, 1): lambda: masks(0),
        (1, 0, 1): lambda: masks(1),
        (1, 1, 0): lambda: masks(2),
        (0, 2, 1): plane1,
        (2, 1, 1): plane2,
        (3, 1, 1): plane3,
        (4, 1, 1): plane4,
        (5, 1, 1): plane5,
        (6, 1, 1): plane6,
        (9, 2, 1): lambda: relays(0, 2),
        (10, 1, 1): lambda: relays(0, 4),
    }
    weights_in = (6, 2, 0)
    done = [0] * CHUNKS
    have = [0] * CHUNKS
    ended = 0
    for t in range(8 + START[-1]):
        for ch in sorted(range(CHUNKS), key=lambda ch: t - START[ch] >= 8):
            step = t - START[ch]
            if step == 8:
                last_arrivals(ch)
                have[ch] = NZ
            for h in (0, 1):
                if 0 <= step < 8:
                    ring(ch, step, h)
                    if h == 1:
                        have[ch] = 2 * step + 1
                if (t, ch, h) >= weights_in and (0 <= step < 8 or step == 8 and h == 1):
                    for _ in range(2):
                        at = done[ended]
                        if all(done[k] == at and have[k] > at for k in range(ended, CHUNKS)):
                            multiply(slice(FROM[ended], ROWS), at, at + 1)
                            done[ended:] = [at + 1] * (CHUNKS - ended)
                if step == 8 and h == 1:
                    multiply(slice(FROM[ch], FROM[ch] + SIZES[ch]), done[ch], NZ)
                    finish(ch)
                    ended = ch + 1
                then.get((t, ch, h), lambda: None)()
    multiply(slice(FROM[2], ROWS), done[2], NZ - 1)
    last_arrivals(2)
    multiply(slice(FROM[2], ROWS), NZ - 1, NZ)
    finish(2)
    kv_arrivals(0)
    attend(0, 0, ROWS)
    kv_arrivals(1)
    attend(1, 0, ROWS)
    kv_arrivals(2)
    attend(2, 0, FROM[2], skip=SIZES[2])
    attend(2, FROM[2], ROWS)

    for d in range(1, NZ):
        square(d).wait_send()
        relay(d).wait_send()
    for k in range(5):
        for d in (1, 3):
            near(k, d).wait_send()
            far(k, d).wait_send()
    for j in range(4):
        for d in range(4):
            to_sibling(j, d).wait_send()

    for ch in range(CHUNKS):
        for step in range(8):
            for h, r in WAYS:
                if is_long(h, r) or step < 7:
                    hop(ch, step, h, r).wait_send()
    for ch in range(CHUNKS):
        if ch in RELAYED:
            for d in (2, 4):
                @pl.when(f + d < 8)
                def _():
                    kv_copy(ch, d).wait_send()

                @pl.when((f >= d) & (f % 2 >= d // 4))
                def _():
                    kv_relay(ch, d).wait_send()

            @pl.when(f % 2 == 0)
            def _():
                kv_copy(ch, 1).wait_send()
        else:
            for d in range(1, BACK + 1):
                @pl.when(f + d < 8)
                def _():
                    kv_copy(ch, d).wait_send()


def hand_over(in_ref, out_ref):
    out_ref[...] = in_ref[...]


def shards(tokens_in, norm_gain, segment_ids, wq, wk, wv):
    vmem = pl.BlockSpec(memory_space=pltpu.VMEM)
    dma = pltpu.SemaphoreType.DMA
    freqs = 500000.0 ** (-(np.arange(HD) % 64) / 64.0)
    hbm = pl.BlockSpec(memory_space=pl.ANY)
    attended = pl.pallas_call(
        front,
        name="front",
        out_shape=jax.ShapeDtypeStruct((ROWS, 512), BF16),
        in_specs=[hbm, vmem] + [hbm] * 5,
        out_specs=vmem,
        scratch_shapes=[
            pltpu.VMEM((ROWS, FEAT), BF16),
            pltpu.VMEM((1, 8 * ROWS), jnp.int32),
            pltpu.VMEM((1, HD), F32),
            pltpu.VMEM((16, 8192), F32),
            pltpu.VMEM((16, 1024), F32),
            pltpu.VMEM((16, 1024), F32),
            pltpu.VMEM((NZ, 16, COLS), BF16),
            pltpu.VMEM((32, 256, COLS), BF16),
            pltpu.VMEM((NZ, ROWS, FEAT), BF16),
            pltpu.VMEM((NZ, 1, ROWS), F32),
            pltpu.VMEM((ROWS, COLS), F32),
            pltpu.VMEM((2, ROWS, HD), F32),
            pltpu.VMEM(((BACK + 1) * ROWS, 3 * HD), BF16),
            pltpu.VMEM((4, ROWS, HD), BF16),
            *[pltpu.VMEM((ROWS, (BACK + 1) * size), F32) for size in SIZES],
            pltpu.VMEM((4, ROWS, HD), F32),
            pltpu.VMEM((4, ROWS, 2 * HD), F32),
            dma((6,)),
            dma((NZ,)), dma((NZ,)),
            dma((NZ,)), dma((NZ,)),
            dma((20,)), dma((20,)),
            dma((16,)), dma((16,)),
            dma((2, CHUNKS * 16)), dma((2, CHUNKS * 16)),
            dma((CHUNKS * 4,)), dma((CHUNKS * 4,)), dma((CHUNKS * 2,)),
        ],
        compiler_params=pltpu.CompilerParams(collective_id=1, has_side_effects=True, vmem_limit_bytes=56 << 20),
        cost_estimate=pl.CostEstimate(flops=2 * ROWS * 8192 * COLS, bytes_accessed=4 << 20, transcendentals=0),
    )(tokens_in, norm_gain, segment_ids, jnp.asarray(freqs[None], F32), wq, wk, wv)
    return pl.pallas_call(
        hand_over,
        name="hand_over",
        out_shape=jax.ShapeDtypeStruct((ROWS, 512), BF16),
        in_specs=[vmem],
        out_specs=vmem,
    )(attended)


def solution(mesh):
    placed = (
        P(("group", "fsdp"), "tensor"),
        P("tensor"),
        P("group", None),
        P(("group", "fsdp", "tensor"), None),
        P(("group", "fsdp", "tensor"), None),
        P(("group", "fsdp", "tensor"), None),
    )
    return jax.shard_map(
        shards,
        mesh=mesh,
        in_specs=placed,
        out_specs=P(("group", "fsdp"), "tensor"),
        check_vma=False,
    )
```
